32 devices in a mesh: dp: 16 (over z, y, x), tensor: 2 (over core).
Axes of the slice: x: 2, y: 2, z: 4, core: 2. Of those that a mesh axis runs over, the one named last changes fastest.
Arguments:
- activations: bfloat16 [2560, 16384], P('dp', 'tensor'), may hold values from -6 to 6
- out_grads: bfloat16 [2560, 53248], P('dp', 'tensor'), may hold values from -6 to 6
- basis_in: bfloat16 [53248, 64], P('tensor'), may hold values from -6 to 6
Outputs:
- left_basis: float32 [16384, 64], P('tensor')
- basis_out: bfloat16 [53248, 64], P('tensor')
The draws below stay inside these ranges and needn't reach their ends.
All inputs are finite; a program needn't handle non-finite values.
Results may differ from the reference program's by a relative error of at most 0.014.
Values may be sent and summed in bfloat16 or wider, within the bound.
A program may use at most 128 MiB of HBM per device.

```python
import jax
import jax.numpy as jnp
from jax import lax

D = 16384
FF = 53248
RANK = 64
TOKENS = 2560


def shard_levels(stream_key, dims, shards, least, largest):
    def one(position, blocks):
        heights = jax.random.uniform(jax.random.fold_in(jax.random.fold_in(stream_key, 6), position), (blocks,), jnp.float32, least / len(shards), largest / len(shards))
        return jnp.repeat(jnp.exp(heights), dims[position] // blocks).reshape((-1,) + (1,) * (len(dims) - position - 1))

    loudness = one(*shards[0])
    for cut in shards[1:]:
        loudness = loudness * one(*cut)
    return loudness


def gaussian(rng, extent, scale, most, cuts=(), kind=jnp.bfloat16):
    entries = scale * jax.random.normal(rng, extent, jnp.float32)
    if cuts:
        entries = entries * shard_levels(rng, extent, cuts, -0.22, 0.18)
    return jnp.clip(entries, -most, most).astype(kind)


def setup_inputs(seed: int = 0) -> dict:
    keys = jax.random.split(jax.random.key(seed), 4)
    activations = gaussian(keys[0], (TOKENS, D), 1.0, 6.0, ((0, 16), (1, 2)))
    out_grads = gaussian(keys[1], (TOKENS, FF), 1.0, 6.0, ((0, 16), (1, 2)))
    basis_in = gaussian(keys[2], (FF, RANK), 1.0, 6.0, ((0, 2),))
    return dict(activations=activations, out_grads=out_grads, basis_in=basis_in)


def orthonormal(block, width):
    gram = jnp.dot(block.T, block, precision=lax.Precision.HIGHEST) / width
    chol = jnp.linalg.cholesky(gram)
    return jax.scipy.linalg.solve_triangular(chol, block.T, lower=True).T

def reference(activations, out_grads, basis_in):
    proj = jnp.dot(out_grads.astype(jnp.float32), basis_in.astype(jnp.float32), preferred_element_type=jnp.float32).astype(jnp.bfloat16)
    left = lax.dot_general(activations.astype(jnp.float32), proj.astype(jnp.float32), (((0,), (0,)), ((), ())), preferred_element_type=jnp.float32)
    left_basis = orthonormal(left, D)
    back = jnp.dot(activations.astype(jnp.float32), left_basis.astype(jnp.bfloat16).astype(jnp.float32), preferred_element_type=jnp.float32).astype(jnp.bfloat16)
    right = lax.dot_general(out_grads.astype(jnp.float32), back.astype(jnp.float32), (((0,), (0,)), ((), ())), preferred_element_type=jnp.float32)
    basis_out = orthonormal(right, FF).astype(jnp.bfloat16)
    return (left_basis, basis_out)
```

```python
import functools

import jax
import jax.numpy as jnp
from jax import lax
from jax.experimental import pallas as pl
from jax.experimental.pallas import tpu as pltpu
from jax.sharding import PartitionSpec as P

LANES = 128
STREAMS = 3


def log2_of(n):
    k = n.bit_length() - 1
    return k if n == 1 << k else None


def plan_streams(width, n):
    k = log2_of(n)
    units = width // (n * LANES)
    streams, offset = [], 0
    for q in range(STREAMS):
        mine = units // STREAMS + (1 if q < units % STREAMS else 0)
        if mine == 0:
            continue
        bits = list(range(k - 1))
        turn = q % max(k - 1, 1)
        order = bits[turn:] + bits[:turn] + [k - 1]
        streams.append((offset, mine * n * LANES, order))
        offset += mine * n * LANES
    return streams


def cholqr_kernel(n, tensors, streams, width, part_ref, out_ref, *scratch):
    k, kt = log2_of(n), log2_of(tensors)
    stages = len(streams) * k
    recv = scratch[:stages]
    whole, gram_out, gram_in, elim = scratch[stages:stages + 4]
    rs_send, rs_recv, ag_send, ag_recv, g_send, g_recv = scratch[stages + 4:]
    rank = part_ref.shape[0]
    me = lax.axis_index("dp")
    core = lax.axis_index("tensor")

    def bit_of(b):
        return lax.rem(me // (1 << b), 2)

    def partner(b):
        return me + (1 << b) - 2 * (1 << b) * bit_of(b)

    def core_partner(b):
        bit = lax.rem(core // (1 << b), 2)
        return core + (1 << b) - 2 * (1 << b) * bit

    targets = [{"dp": partner(b)} for b in range(k)]
    targets += [{"tensor": core_partner(b)} for b in range(kt)]
    barrier = pltpu.get_barrier_semaphore()
    for target in targets:
        pl.semaphore_signal(barrier, inc=1, device_id=target, device_id_type=pl.DeviceIdType.MESH)
    pl.semaphore_wait(barrier, k + kt)

    def remote(src, dst, send, arrive, target):
        return pltpu.make_async_remote_copy(
            src_ref=src, dst_ref=dst, send_sem=send, recv_sem=arrive,
            device_id=target, device_id_type=pl.DeviceIdType.MESH,
        )

    def lanes(start, size):
        return pl.ds(pl.multiple_of(start, LANES), size)

    def rs_copy(q, s):
        offset, wide, order = streams[q]
        half = wide >> (s + 1)
        base = offset if s == 0 else 0
        src = part_ref if s == 0 else recv[q * k + s - 1]
        start = base + (1 - bit_of(order[s])) * half
        return remote(
            src.at[:, lanes(start, half)], recv[q * k + s],
            rs_send.at[q, s], rs_recv.at[q, s], targets[order[s]],
        )

    for q in range(len(streams)):
        rs_copy(q, 0).start()
    for s in range(k):
        for q, (offset, wide, order) in enumerate(streams):
            rs_copy(q, s).wait()
            half = wide >> (s + 1)
            tile = wide // n
            src = part_ref if s == 0 else recv[q * k + s - 1]
            start = (offset if s == 0 else 0) + bit_of(order[s]) * half
            here = recv[q * k + s]

            def add(i, _, src=src, here=here, start=start, tile=tile):
                to = lanes(i * tile, tile)
                mine = src[:, lanes(start + i * tile, tile)].astype(jnp.float32)
                here[:, to] = (mine + here[:, to].astype(jnp.float32)).astype(here.dtype)
                return 0

            lax.fori_loop(0, half // tile, add, 0)
            if s + 1 < k:
                rs_copy(q, s + 1).start()

    def place(q, s):
        offset, wide, order = streams[q]
        start = offset
        for j in range(s):
            start = start + bit_of(order[j]) * (wide >> (j + 1))
        return start

    def other(q, s):
        order = streams[q][2]
        half = streams[q][1] >> (s + 1)
        return place(q, s) + (1 - bit_of(order[s])) * half

    def ag_copy(q, s):
        offset, wide, order = streams[q]
        here = whole.at[:, lanes(place(q, s + 1), wide >> (s + 1))]
        return remote(here, here, ag_send.at[q, s], ag_recv.at[q, s], targets[order[s]])

    gram = jnp.zeros((rank, rank), jnp.float32)
    for q, (offset, wide, order) in enumerate(streams):
        chunk = recv[q * k + k - 1][...]
        whole[:, lanes(place(q, k), wide // n)] = chunk
        ag_copy(q, k - 1).start()
        gram = gram + lax.dot_general(
            chunk, chunk, (((1,), (1,)), ((), ())), preferred_element_type=jnp.float32
        )

    def ag_step(s):
        for q in range(len(streams)):
            ag_copy(q, s).wait()
            if s > 0:
                ag_copy(q, s - 1).start()

    for j in range(k + kt):
        target = targets[(j + k) % (k + kt)]
        gram_out[j] = gram
        copy = remote(gram_out.at[j], gram_in.at[j], g_send.at[j], g_recv.at[j], target)
        copy.start()
        copy.wait()
        gram = gram + gram_in[j]

    gram = gram / width
    row = lax.broadcasted_iota(jnp.int32, (rank, rank), 0)
    col = lax.broadcasted_iota(jnp.int32, (rank, rank), 1)
    elim[:, :rank] = gram
    elim[:, rank:] = jnp.where(row == col, 1.0, 0.0).astype(jnp.float32)
    wide_lane = lax.broadcasted_iota(jnp.int32, (rank, 2 * rank), 1)
    tall_row = lax.broadcasted_iota(jnp.int32, (rank, 1), 0)

    def eliminate(i, _):
        x = elim[...]
        pivot_row = elim[pl.ds(i, 1), :]
        column = jnp.sum(jnp.where(wide_lane == i, x, 0.0), axis=1, keepdims=True)
        pivot = jnp.sum(jnp.where(wide_lane[:1] == i, pivot_row, 0.0), axis=1, keepdims=True)
        factor = jnp.where(tall_row > i, column / pivot, 0.0)
        elim[...] = x - factor * pivot_row
        return 0

    cuts = [rank * j // (k - 1) for j in range(k)]
    for j in range(k - 1):
        ag_step(k - 1 - j)
        lax.fori_loop(cuts[j], cuts[j + 1], eliminate, 0)
    done = elim[...]
    diagonal = jnp.sum(jnp.where(row == col, done[:, :rank], 0.0), axis=1, keepdims=True)
    inverse = done[:, rank:] / jnp.sqrt(diagonal)
    high = inverse.astype(jnp.bfloat16)
    low = (inverse - high.astype(jnp.float32)).astype(jnp.bfloat16)

    def apply(start, size, tile):
        def step(i, _):
            at = lanes(start + i * tile, tile)
            rows = whole[:, at]
            out_ref[:, at] = (
                jnp.dot(high, rows, preferred_element_type=jnp.float32)
                + jnp.dot(low, rows, preferred_element_type=jnp.float32)
            ).astype(out_ref.dtype)
            return 0

        lax.fori_loop(0, size // tile, step, 0)

    for q, (offset, wide, order) in enumerate(streams):
        apply(place(q, 1), wide // 2, wide // n)
    ag_step(0)
    for q, (offset, wide, order) in enumerate(streams):
        apply(other(q, 0), wide // 2, wide // n)


def cholqr(part, n, tensors, width, dtype, collective_id):
    rank, local = part.shape
    k, kt = log2_of(n), log2_of(tensors)
    streams = plan_streams(local, n)
    recv = [
        pltpu.VMEM((rank, wide >> (s + 1)), jnp.bfloat16)
        for _, wide, _ in streams
        for s in range(k)
    ]
    dma = pltpu.SemaphoreType.DMA
    return pl.pallas_call(
        functools.partial(cholqr_kernel, n, tensors, streams, width),
        out_shape=jax.ShapeDtypeStruct((rank, local), dtype),
        in_specs=[pl.BlockSpec(memory_space=pltpu.VMEM)],
        out_specs=pl.BlockSpec(memory_space=pltpu.VMEM),
        scratch_shapes=recv + [
            pltpu.VMEM((rank, local), jnp.bfloat16),
            pltpu.VMEM((k + kt, rank, rank), jnp.float32),
            pltpu.VMEM((k + kt, rank, rank), jnp.float32),
            pltpu.VMEM((rank, 2 * rank), jnp.float32),
            dma((len(streams), k)), dma((len(streams), k)),
            dma((len(streams), k)), dma((len(streams), k)),
            dma((k + kt,)), dma((k + kt,)),
        ],
        compiler_params=pltpu.CompilerParams(
            collective_id=collective_id, has_side_effects=True,
            vmem_limit_bytes=32 * 1024 * 1024,
        ),
    )(part)


def plain_cholqr(part, width):
    total = lax.psum(part, "dp")
    gram = lax.psum(
        jnp.dot(total, total.T, precision=lax.Precision.HIGHEST), "tensor"
    )
    chol = jnp.linalg.cholesky(gram / width)
    return jax.scipy.linalg.solve_triangular(chol, total, lower=True)


def per_device(n, tensors, activations, out_grads, basis_in):
    def basis(part, dtype, collective_id):
        width = part.shape[1] * tensors
        k, kt = log2_of(n), log2_of(tensors)
        if k is None or k < 2 or kt is None or part.shape[1] % (n * LANES):
            return plain_cholqr(part, width).astype(dtype)
        return cholqr(part.astype(jnp.bfloat16), n, tensors, width, dtype, collective_id)

    proj = lax.psum(
        jnp.dot(out_grads, basis_in, preferred_element_type=jnp.float32), "tensor"
    ).astype(jnp.bfloat16)
    left_part = lax.dot_general(
        proj, activations, (((0,), (0,)), ((), ())), preferred_element_type=jnp.float32
    )
    left_basis = basis(left_part, jnp.float32, 0)
    back = lax.psum(
        lax.dot_general(
            activations, left_basis.astype(jnp.bfloat16), (((1,), (1,)), ((), ())),
            preferred_element_type=jnp.float32,
        ).astype(jnp.bfloat16),
        "tensor",
    )
    right_part = lax.dot_general(
        back, out_grads, (((0,), (0,)), ((), ())), preferred_element_type=jnp.float32
    )
    basis_out = basis(right_part, jnp.bfloat16, 1)
    return (left_basis.T, basis_out.T)


def solution(mesh):
    return jax.shard_map(
        functools.partial(per_device, mesh.shape["dp"], mesh.shape["tensor"]),
        mesh=mesh,
        in_specs=(P("dp", "tensor"), P("dp", "tensor"), P("tensor", None)),
        out_specs=(P("tensor", None), P("tensor", None)),
        check_vma=False,
    )
```

```python
import functools

import jax
import jax.numpy as jnp
from jax import lax
from jax.experimental import pallas as pl
from jax.experimental.pallas import tpu as pltpu
from jax.sharding import PartitionSpec as P

LANES = 128
STREAMS = 6


def log2_of(n):
    k = n.bit_length() - 1
    return k if n == 1 << k else None


def plan_streams(width, n):
    k = log2_of(n)
    units = width // (n * LANES)
    streams, offset = [], 0
    for q in range(STREAMS):
        mine = units // STREAMS + (1 if q < units % STREAMS else 0)
        if mine == 0:
            continue
        bits = list(range(k - 1))
        turn = q % (k - 1)
        order = bits[turn:] + bits[:turn] + [k - 1]
        streams.append((offset, mine * n * LANES, order))
        offset += mine * n * LANES
    return streams


def cholqr_kernel(n, tensors, streams, width, part_ref, out_ref, *scratch):
    k, kt = log2_of(n), log2_of(tensors)
    stages = len(streams) * k
    recv = scratch[:stages]
    whole, gram_out, gram_in, elim = scratch[stages:stages + 4]
    rs_send, rs_recv, ag_send, ag_recv, g_send, g_recv = scratch[stages + 4:]
    rank = part_ref.shape[0]
    me = lax.axis_index("dp")
    core = lax.axis_index("tensor")

    def bit_of(b):
        return lax.rem(me // (1 << b), 2)

    def partner(b):
        return me + (1 << b) - 2 * (1 << b) * bit_of(b)

    def core_partner(b):
        bit = lax.rem(core // (1 << b), 2)
        return core + (1 << b) - 2 * (1 << b) * bit

    targets = [{"dp": partner(b)} for b in range(k)]
    targets += [{"tensor": core_partner(b)} for b in range(kt)]
    barrier = pltpu.get_barrier_semaphore()
    for target in targets:
        pl.semaphore_signal(barrier, inc=1, device_id=target, device_id_type=pl.DeviceIdType.MESH)
    pl.semaphore_wait(barrier, k + kt)

    def remote(src, dst, send, arrive, target):
        return pltpu.make_async_remote_copy(
            src_ref=src, dst_ref=dst, send_sem=send, recv_sem=arrive,
            device_id=target, device_id_type=pl.DeviceIdType.MESH,
        )

    def lanes(start, size):
        return pl.ds(pl.multiple_of(start, LANES), size)

    def rs_copy(q, s):
        offset, wide, order = streams[q]
        half = wide >> (s + 1)
        base = offset if s == 0 else 0
        src = part_ref if s == 0 else recv[q * k + s - 1]
        start = base + (1 - bit_of(order[s])) * half
        return remote(
            src.at[:, lanes(start, half)], recv[q * k + s],
            rs_send.at[q, s], rs_recv.at[q, s], targets[order[s]],
        )

    for q in range(len(streams)):
        rs_copy(q, 0).start()
    for s in range(k):
        for q, (offset, wide, order) in enumerate(streams):
            rs_copy(q, s).wait_recv()
            half = wide >> (s + 1)
            tile = wide // n
            src = part_ref if s == 0 else recv[q * k + s - 1]
            start = (offset if s == 0 else 0) + bit_of(order[s]) * half
            here = recv[q * k + s]

            def add(i, _, src=src, here=here, start=start, tile=tile):
                to = lanes(i * tile, tile)
                mine = src[:, lanes(start + i * tile, tile)].astype(jnp.float32)
                here[:, to] = (mine + here[:, to].astype(jnp.float32)).astype(here.dtype)
                return 0

            lax.fori_loop(0, half // tile, add, 0)
            if s + 1 < k:
                rs_copy(q, s + 1).start()

    def place(q, s):
        offset, wide, order = streams[q]
        start = offset
        for j in range(s):
            start = start + bit_of(order[j]) * (wide >> (j + 1))
        return start

    def other(q, s):
        order = streams[q][2]
        half = streams[q][1] >> (s + 1)
        return place(q, s) + (1 - bit_of(order[s])) * half

    def ag_copy(q, s):
        offset, wide, order = streams[q]
        here = whole.at[:, lanes(place(q, s + 1), wide >> (s + 1))]
        return remote(here, here, ag_send.at[q, s], ag_recv.at[q, s], targets[order[s]])

    gram = jnp.zeros((rank, rank), jnp.float32)
    for q, (offset, wide, order) in enumerate(streams):
        chunk = recv[q * k + k - 1][...]
        whole[:, lanes(place(q, k), wide // n)] = chunk
        ag_copy(q, k - 1).start()
        gram = gram + lax.dot_general(
            chunk, chunk, (((1,), (1,)), ((), ())), preferred_element_type=jnp.float32
        )

    def ag_step(s):
        for q in range(len(streams)):
            ag_copy(q, s).wait_recv()
            if s > 0:
                ag_copy(q, s - 1).start()

    def gram_copy(j):
        return remote(
            gram_out.at[j], gram_in.at[j], g_send.at[j], g_recv.at[j],
            targets[(j + k) % (k + kt)],
        )

    gram_out[0] = gram
    gram_copy(0).start()
    gathered = k - 1
    for j in range(k + kt):
        gram_copy(j).wait_recv()
        gram = gram + gram_in[j]
        if j + 1 < k + kt:
            gram_out[j + 1] = gram
            gram_copy(j + 1).start()
        if j % 2 == 1 and gathered > 1:
            ag_step(gathered)
            gathered -= 1

    gram = gram / width
    row = lax.broadcasted_iota(jnp.int32, (rank, rank), 0)
    col = lax.broadcasted_iota(jnp.int32, (rank, rank), 1)
    elim[:, :rank] = gram
    elim[:, rank:] = jnp.where(row == col, 1.0, 0.0).astype(jnp.float32)
    wide_lane = lax.broadcasted_iota(jnp.int32, (rank, 2 * rank), 1)
    tall_row = lax.broadcasted_iota(jnp.int32, (rank, 1), 0)

    def eliminate(i, _):
        x = elim[...]
        pivot_row = elim[pl.ds(i, 1), :]
        column = jnp.sum(jnp.where(wide_lane == i, x, 0.0), axis=1, keepdims=True)
        pivot = jnp.sum(jnp.where(wide_lane[:1] == i, pivot_row, 0.0), axis=1, keepdims=True)
        factor = jnp.where(tall_row > i, column / pivot, 0.0)
        elim[...] = x - factor * pivot_row
        return 0

    cuts = [rank * j // (gathered + 1) for j in range(gathered + 2)]
    for j in range(gathered + 1):
        lax.fori_loop(cuts[j], cuts[j + 1], eliminate, 0)
        if gathered - j > 0:
            ag_step(gathered - j)
    done = elim[...]
    diagonal = jnp.sum(jnp.where(row == col, done[:, :rank], 0.0), axis=1, keepdims=True)
    inverse = done[:, rank:] / jnp.sqrt(diagonal)
    high = inverse.astype(jnp.bfloat16)
    low = (inverse - high.astype(jnp.float32)).astype(jnp.bfloat16)
    both = jnp.concatenate([high, low], axis=0)
    tile = n // 2 * LANES

    def apply(start, size):
        def step(i, _):
            at = lanes(start + i * tile, tile)
            two = jnp.dot(both, whole[:, at], preferred_element_type=jnp.float32)
            out_ref[:, at] = (two[:rank] + two[rank:]).astype(out_ref.dtype)
            return 0

        lax.fori_loop(0, size // tile, step, 0)

    for q, (offset, wide, order) in enumerate(streams):
        apply(place(q, 1), wide // 2)
    ag_step(0)
    for q, (offset, wide, order) in enumerate(streams):
        apply(other(q, 0), wide // 2)
    for q in range(len(streams)):
        for s in range(k):
            rs_copy(q, s).wait_send()
            ag_copy(q, s).wait_send()
    for j in range(k + kt):
        gram_copy(j).wait_send()


def cholqr(part, n, tensors, width, dtype, collective_id):
    rank, local = part.shape
    k, kt = log2_of(n), log2_of(tensors)
    streams = plan_streams(local, n)
    recv = [
        pltpu.VMEM((rank, wide >> (s + 1)), jnp.bfloat16)
        for _, wide, _ in streams
        for s in range(k)
    ]
    dma = pltpu.SemaphoreType.DMA
    return pl.pallas_call(
        functools.partial(cholqr_kernel, n, tensors, streams, width),
        out_shape=jax.ShapeDtypeStruct((rank, local), dtype),
        in_specs=[pl.BlockSpec(memory_space=pltpu.VMEM)],
        out_specs=pl.BlockSpec(memory_space=pltpu.VMEM),
        scratch_shapes=recv + [
            pltpu.VMEM((rank, local), jnp.bfloat16),
            pltpu.VMEM((k + kt, rank, rank), jnp.float32),
            pltpu.VMEM((k + kt, rank, rank), jnp.float32),
            pltpu.VMEM((rank, 2 * rank), jnp.float32),
            dma((len(streams), k)), dma((len(streams), k)),
            dma((len(streams), k)), dma((len(streams), k)),
            dma((k + kt,)), dma((k + kt,)),
        ],
        compiler_params=pltpu.CompilerParams(
            collective_id=collective_id, has_side_effects=True,
            vmem_limit_bytes=32 * 1024 * 1024,
        ),
    )(part)


def plain_cholqr(part, width):
    total = lax.psum(part, "dp")
    gram = lax.psum(
        jnp.dot(total, total.T, precision=lax.Precision.HIGHEST), "tensor"
    )
    chol = jnp.linalg.cholesky(gram / width)
    return jax.scipy.linalg.solve_triangular(chol, total, lower=True)


def per_device(n, tensors, activations, out_grads, basis_in):
    def basis(part, dtype, collective_id):
        width = part.shape[1] * tensors
        k, kt = log2_of(n), log2_of(tensors)
        if k is None or k < 2 or kt is None or part.shape[1] % (n * LANES):
            return plain_cholqr(part, width).astype(dtype)
        return cholqr(part.astype(jnp.bfloat16), n, tensors, width, dtype, collective_id)

    proj = lax.psum(
        jnp.dot(out_grads, basis_in, preferred_element_type=jnp.float32), "tensor"
    ).astype(jnp.bfloat16)
    left_part = lax.dot_general(
        proj, activations, (((0,), (0,)), ((), ())), preferred_element_type=jnp.float32
    )
    left_basis = basis(left_part, jnp.float32, 0)
    back = lax.psum(
        lax.dot_general(
            activations, left_basis.astype(jnp.bfloat16), (((1,), (1,)), ((), ())),
            preferred_element_type=jnp.float32,
        ).astype(jnp.bfloat16),
        "tensor",
    )
    right_part = lax.dot_general(
        back, out_grads, (((0,), (0,)), ((), ())), preferred_element_type=jnp.float32
    )
    basis_out = basis(right_part, jnp.bfloat16, 1)
    return (left_basis.T, basis_out.T)


def solution(mesh):
    return jax.shard_map(
        functools.partial(per_device, mesh.shape["dp"], mesh.shape["tensor"]),
        mesh=mesh,
        in_specs=(P("dp", "tensor"), P("dp", "tensor"), P("tensor", None)),
        out_specs=(P("tensor", None), P("tensor", None)),
        check_vma=False,
    )
```

```python
import functools

import jax
import jax.numpy as jnp
from jax import lax
from jax.experimental import pallas as pl
from jax.experimental.pallas import tpu as pltpu
from jax.sharding import PartitionSpec as P

LANES = 128
STREAMS = 6


def log2_of(n):
    k = n.bit_length() - 1
    return k if n == 1 << k else None


def plan_streams(width, n):
    k = log2_of(n)
    units = width // (n * LANES)
    streams, offset = [], 0
    for q in range(STREAMS):
        mine = units // STREAMS + (1 if q < units % STREAMS else 0)
        if mine == 0:
            continue
        bits = list(range(k - 1))
        turn = q % (k - 1)
        order = bits[turn:] + bits[:turn] + [k - 1]
        streams.append((offset, mine * n * LANES, order))
        offset += mine * n * LANES
    return streams


def power_kernel(
    n, tensors, sides, act_hbm, grad_hbm, left_part, left_out, right_out, *scratch
):
    k, kt = log2_of(n), log2_of(tensors)
    scratch = list(scratch)

    def take(count):
        taken = scratch[:count]
        del scratch[:count]
        return taken

    recvs = [take(len(streams) * k) for streams, _ in sides]
    left_whole, right_whole, right_part = take(3)
    gram_out, gram_in, elim, back_out, back_in, act, grad = take(7)
    side_sems = [take(6) for _ in sides]
    b_send, b_recv, load = take(3)
    rank = left_part.shape[0]
    me = lax.axis_index("dp")
    core = lax.axis_index("tensor")

    act_load = pltpu.make_async_copy(act_hbm, act, load.at[0])
    grad_load = pltpu.make_async_copy(grad_hbm, grad, load.at[1])
    act_load.start()
    grad_load.start()

    def bit_of(b):
        return lax.rem(me // (1 << b), 2)

    def partner(b):
        return me + (1 << b) - 2 * (1 << b) * bit_of(b)

    def core_partner(b):
        bit = lax.rem(core // (1 << b), 2)
        return core + (1 << b) - 2 * (1 << b) * bit

    targets = [{"dp": partner(b)} for b in range(k)]
    targets += [{"tensor": core_partner(b)} for b in range(kt)]
    barrier = pltpu.get_barrier_semaphore()
    for target in targets:
        pl.semaphore_signal(barrier, inc=1, device_id=target, device_id_type=pl.DeviceIdType.MESH)
    pl.semaphore_wait(barrier, k + kt)

    def remote(src, dst, send, arrive, target):
        return pltpu.make_async_remote_copy(
            src_ref=src, dst_ref=dst, send_sem=send, recv_sem=arrive,
            device_id=target, device_id_type=pl.DeviceIdType.MESH,
        )

    def lanes(start, size):
        return pl.ds(pl.multiple_of(start, LANES), size)

    tile = n // 2 * LANES

    def tiles(start, size, body):
        def step(i, _):
            body(lanes(start + i * tile, tile))
            return 0

        lax.fori_loop(0, size // tile, step, 0)

    row = lax.broadcasted_iota(jnp.int32, (rank, rank), 0)
    col = lax.broadcasted_iota(jnp.int32, (rank, rank), 1)
    wide_lane = lax.broadcasted_iota(jnp.int32, (rank, 2 * rank), 1)
    tall_row = lax.broadcasted_iota(jnp.int32, (rank, 1), 0)

    def eliminate(i, _):
        x = elim[...]
        pivot_row = elim[pl.ds(i, 1), :]
        column = jnp.sum(jnp.where(wide_lane == i, x, 0.0), axis=1, keepdims=True)
        pivot = jnp.sum(jnp.where(wide_lane[:1] == i, pivot_row, 0.0), axis=1, keepdims=True)
        factor = jnp.where(tall_row > i, column / pivot, 0.0)
        elim[...] = x - factor * pivot_row
        return 0

    def cholqr(side, part, whole, produce, beside, arrived):
        streams, width = sides[side]
        recv = recvs[side]
        rs_send, rs_recv, ag_send, ag_recv, g_send, g_recv = side_sems[side]
        count = len(streams)

        def rs_copy(q, s):
            offset, wide, order = streams[q]
            half = wide >> (s + 1)
            src = part if s == 0 else recv[q * k + s - 1]
            start = (offset if s == 0 else 0) + (1 - bit_of(order[s])) * half
            return remote(
                src.at[:, lanes(start, half)], recv[q * k + s],
                rs_send.at[q, s], rs_recv.at[q, s], targets[order[s]],
            )

        for q, (offset, wide, order) in enumerate(streams):
            produce(offset + (1 - bit_of(order[0])) * (wide // 2), wide // 2)
            rs_copy(q, 0).start()
        for q, (offset, wide, order) in enumerate(streams):
            produce(offset + bit_of(order[0]) * (wide // 2), wide // 2)
        beside()
        for s in range(k):
            for q, (offset, wide, order) in enumerate(streams):
                rs_copy(q, s).wait_recv()
                half = wide >> (s + 1)
                step = wide // n
                src = part if s == 0 else recv[q * k + s - 1]
                start = (offset if s == 0 else 0) + bit_of(order[s]) * half
                here = recv[q * k + s]

                def add(i, _, src=src, here=here, start=start, step=step):
                    to = lanes(i * step, step)
                    mine = src[:, lanes(start + i * step, step)].astype(jnp.float32)
                    here[:, to] = (mine + here[:, to].astype(jnp.float32)).astype(here.dtype)
                    return 0

                lax.fori_loop(0, half // step, add, 0)
                if s + 1 < k:
                    rs_copy(q, s + 1).start()

        def place(q, s):
            offset, wide, order = streams[q]
            start = offset
            for j in range(s):
                start = start + bit_of(order[j]) * (wide >> (j + 1))
            return start

        def ag_copy(q, s):
            offset, wide, order = streams[q]
            here = whole.at[:, lanes(place(q, s + 1), wide >> (s + 1))]
            return remote(here, here, ag_send.at[q, s], ag_recv.at[q, s], targets[order[s]])

        gram = jnp.zeros((rank, rank), jnp.float32)
        for q, (offset, wide, order) in enumerate(streams):
            chunk = recv[q * k + k - 1][...]
            whole[:, lanes(place(q, k), wide // n)] = chunk
            ag_copy(q, k - 1).start()
            gram = gram + lax.dot_general(
                chunk, chunk, (((1,), (1,)), ((), ())), preferred_element_type=jnp.float32
            )

        def ag_step(s):
            for q in range(count):
                ag_copy(q, s).wait_recv()
                if s > 0:
                    ag_copy(q, s - 1).start()

        def gram_copy(j):
            return remote(
                gram_out.at[side, j], gram_in.at[side, j], g_send.at[j], g_recv.at[j],
                targets[(j + k) % (k + kt)],
            )

        gram_out[side, 0] = gram
        gram_copy(0).start()
        gathered = k - 1
        for j in range(k + kt):
            gram_copy(j).wait_recv()
            gram = gram + gram_in[side, j]
            if j + 1 < k + kt:
                gram_out[side, j + 1] = gram
                gram_copy(j + 1).start()
            if j % 2 == 1 and gathered > 1:
                ag_step(gathered)
                gathered -= 1

        elim[:, :rank] = gram / width
        elim[:, rank:] = jnp.where(row == col, 1.0, 0.0).astype(jnp.float32)
        cuts = [rank * j // (gathered + 1) for j in range(gathered + 2)]
        for j in range(gathered + 1):
            lax.fori_loop(cuts[j], cuts[j + 1], eliminate, 0)
            if gathered - j > 0:
                ag_step(gathered - j)
        done = elim[...]
        diagonal = jnp.sum(jnp.where(row == col, done[:, :rank], 0.0), axis=1, keepdims=True)
        inverse = done[:, rank:] / jnp.sqrt(diagonal)
        finish = arrived(inverse)
        for q, (offset, wide, order) in enumerate(streams):
            finish(place(q, 1), wide // 2)
        ag_step(0)
        for q, (offset, wide, order) in enumerate(streams):
            finish(place(q, 0) + (1 - bit_of(order[0])) * (wide // 2), wide // 2)
        for q in range(count):
            for s in range(k):
                rs_copy(q, s).wait_send()
                ag_copy(q, s).wait_send()
        for j in range(k + kt):
            gram_copy(j).wait_send()
        return inverse

    def halves(inverse):
        high = inverse.astype(jnp.bfloat16)
        low = (inverse - high.astype(jnp.float32)).astype(jnp.bfloat16)
        return jnp.concatenate([high, low], axis=0)

    def apply(inverse, whole, out):
        both = halves(inverse)

        def body(at):
            two = jnp.dot(both, whole[:, at], preferred_element_type=jnp.float32)
            out[:, at] = (two[:rank] + two[rank:]).astype(out.dtype)

        return body

    back_out[0] = jnp.zeros_like(back_out[0])
    act_load.wait()

    def left_arrived(inverse):
        def body(at):
            back_out[0] += lax.dot_general(
                left_whole[:, at], act[:, at], (((1,), (1,)), ((), ())),
                preferred_element_type=jnp.float32,
            )

        return lambda start, size: tiles(start, size, body)

    left_inverse = cholqr(
        0, left_part, left_whole, lambda start, size: None, lambda: None, left_arrived
    )

    def back_copy(j):
        return remote(
            back_out.at[j], back_in.at[j], b_send.at[j], b_recv.at[j], targets[k + j]
        )

    total = back_out[0]
    for j in range(kt):
        if j > 0:
            back_out[j] = total
        back_copy(j).start()
        back_copy(j).wait()
        total = total + back_in[j]
    back = jnp.dot(
        left_inverse, total, precision=lax.Precision.HIGHEST,
        preferred_element_type=jnp.float32,
    ).astype(jnp.bfloat16)

    grad_load.wait()

    def multiply(at):
        right_part[:, at] = jnp.dot(
            back, grad[:, at], preferred_element_type=jnp.float32
        ).astype(right_part.dtype)

    def left_basis():
        tiles(0, left_out.shape[1], apply(left_inverse, left_whole, left_out))

    def right_arrived(inverse):
        body = apply(inverse, right_whole, right_out)
        return lambda start, size: tiles(start, size, body)

    cholqr(
        1, right_part, right_whole,
        lambda start, size: tiles(start, size, multiply), left_basis, right_arrived,
    )


def power_step(left_part, activations, out_grads, n, tensors):
    rank, left_local = left_part.shape
    tokens, right_local = out_grads.shape
    k, kt = log2_of(n), log2_of(tensors)
    locals_ = (left_local, right_local)
    sides = [(plan_streams(local, n), local * tensors) for local in locals_]
    recv = [
        pltpu.VMEM((rank, wide >> (s + 1)), jnp.bfloat16)
        for streams, _ in sides
        for _, wide, _ in streams
        for s in range(k)
    ]
    dma = pltpu.SemaphoreType.DMA
    sems = []
    for streams, _ in sides:
        sems += [dma((len(streams), k))] * 4 + [dma((k + kt,))] * 2
    back_slots = max(kt, 1)
    return pl.pallas_call(
        functools.partial(power_kernel, n, tensors, sides),
        out_shape=(
            jax.ShapeDtypeStruct((rank, left_local), jnp.float32),
            jax.ShapeDtypeStruct((rank, right_local), jnp.bfloat16),
        ),
        in_specs=[
            pl.BlockSpec(memory_space=pl.ANY),
            pl.BlockSpec(memory_space=pl.ANY),
            pl.BlockSpec(memory_space=pltpu.VMEM),
        ],
        out_specs=(
            pl.BlockSpec(memory_space=pltpu.VMEM),
            pl.BlockSpec(memory_space=pltpu.VMEM),
        ),
        scratch_shapes=recv + [
            pltpu.VMEM((rank, left_local), jnp.bfloat16),
            pltpu.VMEM((rank, right_local), jnp.bfloat16),
            pltpu.VMEM((rank, right_local), jnp.bfloat16),
            pltpu.VMEM((2, k + kt, rank, rank), jnp.float32),
            pltpu.VMEM((2, k + kt, rank, rank), jnp.float32),
            pltpu.VMEM((rank, 2 * rank), jnp.float32),
            pltpu.VMEM((back_slots, rank, tokens), jnp.float32),
            pltpu.VMEM((back_slots, rank, tokens), jnp.float32),
            pltpu.VMEM((tokens, left_local), jnp.bfloat16),
            pltpu.VMEM((tokens, right_local), jnp.bfloat16),
        ] + sems + [dma((back_slots,)), dma((back_slots,)), dma((2,))],
        compiler_params=pltpu.CompilerParams(
            collective_id=0, has_side_effects=True,
            vmem_limit_bytes=52 * 1024 * 1024,
        ),
    )(activations, out_grads, left_part)


def plain_cholqr(part, width):
    total = lax.psum(part, "dp")
    gram = lax.psum(
        jnp.dot(total, total.T, precision=lax.Precision.HIGHEST), "tensor"
    )
    chol = jnp.linalg.cholesky(gram / width)
    return jax.scipy.linalg.solve_triangular(chol, total, lower=True)


def plain_step(left_part, activations, out_grads, tensors):
    left_basis = plain_cholqr(left_part, activations.shape[1] * tensors)
    back = lax.psum(
        lax.dot_general(
            activations, left_basis.astype(jnp.bfloat16), (((1,), (1,)), ((), ())),
            preferred_element_type=jnp.float32,
        ).astype(jnp.bfloat16),
        "tensor",
    )
    right_part = lax.dot_general(
        back, out_grads, (((0,), (0,)), ((), ())), preferred_element_type=jnp.float32
    )
    right_basis = plain_cholqr(right_part, out_grads.shape[1] * tensors)
    return left_basis, right_basis.astype(jnp.bfloat16)


def per_device(n, tensors, activations, out_grads, basis_in):
    proj = lax.psum(
        jnp.dot(out_grads, basis_in, preferred_element_type=jnp.float32), "tensor"
    ).astype(jnp.bfloat16)
    left_part = lax.dot_general(
        proj, activations, (((0,), (0,)), ((), ())), preferred_element_type=jnp.float32
    )
    k, kt = log2_of(n), log2_of(tensors)
    aligned = all(x.shape[1] % (n * LANES) == 0 for x in (activations, out_grads))
    if k is None or k < 2 or kt is None or not aligned:
        left_basis, right_basis = plain_step(left_part, activations, out_grads, tensors)
    else:
        left_basis, right_basis = power_step(
            left_part.astype(jnp.bfloat16), activations, out_grads, n, tensors
        )
    return (left_basis.T, right_basis.T)


def solution(mesh):
    return jax.shard_map(
        functools.partial(per_device, mesh.shape["dp"], mesh.shape["tensor"]),
        mesh=mesh,
        in_specs=(P("dp", "tensor"), P("dp", "tensor"), P("tensor", None)),
        out_specs=(P("tensor", None), P("tensor", None)),
        check_vma=False,
    )
```

```python
import functools

import jax
import jax.numpy as jnp
from jax import lax
from jax.experimental import pallas as pl
from jax.experimental.pallas import tpu as pltpu
from jax.sharding import PartitionSpec as P

LANES = 128
STREAMS = 6


def log2_of(n):
    k = n.bit_length() - 1
    return k if n == 1 << k else None


def plan_streams(width, n):
    k = log2_of(n)
    units = width // (n * LANES)
    streams, offset = [], 0
    shares = [units // STREAMS + (q < units % STREAMS) for q in range(STREAMS)]
    if shares[-1] >= 2:
        shares[-1] -= 1
        shares[1] += 1
    for q, mine in enumerate(shares):
        if mine == 0:
            continue
        bits = list(range(k - 1))
        turn = q % (k - 1)
        order = bits[turn:] + bits[:turn] + [k - 1]
        streams.append((offset, mine * n * LANES, order))
        offset += mine * n * LANES
    return streams


def power_kernel(
    n, tensors, sides, act_hbm, grad_hbm, proj_part, left_out, right_out, *scratch
):
    k, kt = log2_of(n), log2_of(tensors)
    scratch = list(scratch)

    def take(count):
        taken = scratch[:count]
        del scratch[:count]
        return taken

    recvs = [take(len(streams) * k) for streams, _ in sides]
    left_whole, left_part, right_whole, right_part = take(4)
    gram_out, gram_in, elim, back_out, back_in, act, grad = take(7)
    side_sems = [take(6) for _ in sides]
    b_send, b_recv, load = take(3)
    rank = proj_part.shape[0]
    me = lax.axis_index("dp")
    core = lax.axis_index("tensor")

    act_load = pltpu.make_async_copy(act_hbm, act, load.at[0])
    grad_load = pltpu.make_async_copy(grad_hbm, grad, load.at[1])
    act_load.start()
    grad_load.start()

    def bit_of(b):
        return lax.rem(me // (1 << b), 2)

    def partner(b):
        return me + (1 << b) - 2 * (1 << b) * bit_of(b)

    def core_partner(b):
        bit = lax.rem(core // (1 << b), 2)
        return core + (1 << b) - 2 * (1 << b) * bit

    targets = [{"dp": partner(b)} for b in range(k)]
    targets += [{"tensor": core_partner(b)} for b in range(kt)]
    barrier = pltpu.get_barrier_semaphore()
    for target in targets:
        pl.semaphore_signal(barrier, inc=1, device_id=target, device_id_type=pl.DeviceIdType.MESH)
    pl.semaphore_wait(barrier, k + kt)

    def remote(src, dst, send, arrive, target):
        return pltpu.make_async_remote_copy(
            src_ref=src, dst_ref=dst, send_sem=send, recv_sem=arrive,
            device_id=target, device_id_type=pl.DeviceIdType.MESH,
        )

    def lanes(start, size):
        return pl.ds(pl.multiple_of(start, LANES), size)

    tile = n // 2 * LANES

    def tiles(start, size, body):
        def step(i, _):
            body(lanes(start + i * tile, tile))
            return 0

        lax.fori_loop(0, size // tile, step, 0)

    row = lax.broadcasted_iota(jnp.int32, (rank, rank), 0)
    col = lax.broadcasted_iota(jnp.int32, (rank, rank), 1)
    wide_lane = lax.broadcasted_iota(jnp.int32, (rank, 2 * rank), 1)
    tall_row = lax.broadcasted_iota(jnp.int32, (rank, 1), 0)

    def eliminate(i, _):
        x = elim[...]
        pivot_row = elim[pl.ds(i, 1), :]
        column = jnp.sum(jnp.where(wide_lane == i, x, 0.0), axis=1, keepdims=True)
        pivot = jnp.sum(jnp.where(wide_lane[:1] == i, pivot_row, 0.0), axis=1, keepdims=True)
        factor = jnp.where(tall_row > i, column / pivot, 0.0)
        elim[...] = x - factor * pivot_row
        return 0

    def cholqr(side, part, whole, produce, beside, arrived):
        streams, width = sides[side]
        recv = recvs[side]
        rs_send, rs_recv, ag_send, ag_recv, g_send, g_recv = side_sems[side]
        count = len(streams)

        def rs_copy(q, s):
            offset, wide, order = streams[q]
            half = wide >> (s + 1)
            src = part if s == 0 else recv[q * k + s - 1]
            start = (offset if s == 0 else 0) + (1 - bit_of(order[s])) * half
            return remote(
                src.at[:, lanes(start, half)], recv[q * k + s],
                rs_send.at[q, s], rs_recv.at[q, s], targets[order[s]],
            )

        for q, (offset, wide, order) in enumerate(streams):
            produce(offset + (1 - bit_of(order[0])) * (wide // 2), wide // 2)
            rs_copy(q, 0).start()
        for q, (offset, wide, order) in enumerate(streams):
            produce(offset + bit_of(order[0]) * (wide // 2), wide // 2)
        beside()
        for s in range(k):
            for q, (offset, wide, order) in enumerate(streams):
                rs_copy(q, s).wait_recv()
                half = wide >> (s + 1)
                step = wide // n
                src = part if s == 0 else recv[q * k + s - 1]
                start = (offset if s == 0 else 0) + bit_of(order[s]) * half
                here = recv[q * k + s]

                def add(i, _, src=src, here=here, start=start, step=step):
                    to = lanes(i * step, step)
                    mine = src[:, lanes(start + i * step, step)].astype(jnp.float32)
                    here[:, to] = (mine + here[:, to].astype(jnp.float32)).astype(here.dtype)
                    return 0

                lax.fori_loop(0, half // step, add, 0)
                if s + 1 < k:
                    rs_copy(q, s + 1).start()

        def place(q, s):
            offset, wide, order = streams[q]
            start = offset
            for j in range(s):
                start = start + bit_of(order[j]) * (wide >> (j + 1))
            return start

        def ag_copy(q, s):
            offset, wide, order = streams[q]
            here = whole.at[:, lanes(place(q, s + 1), wide >> (s + 1))]
            return remote(here, here, ag_send.at[q, s], ag_recv.at[q, s], targets[order[s]])

        gram = jnp.zeros((rank, rank), jnp.float32)
        for q, (offset, wide, order) in enumerate(streams):
            chunk = recv[q * k + k - 1][...]
            whole[:, lanes(place(q, k), wide // n)] = chunk
            ag_copy(q, k - 1).start()
            gram = gram + lax.dot_general(
                chunk, chunk, (((1,), (1,)), ((), ())), preferred_element_type=jnp.float32
            )

        def ag_step(s):
            for q in range(count):
                ag_copy(q, s).wait_recv()
                if s > 0:
                    ag_copy(q, s - 1).start()

        def gram_copy(j):
            return remote(
                gram_out.at[side, j], gram_in.at[side, j], g_send.at[j], g_recv.at[j],
                targets[(j + k) % (k + kt)],
            )

        gram_out[side, 0] = gram
        gram_copy(0).start()
        gathered = k - 1
        for j in range(k + kt):
            gram_copy(j).wait_recv()
            gram = gram + gram_in[side, j]
            if j + 1 < k + kt:
                gram_out[side, j + 1] = gram
                gram_copy(j + 1).start()
            if j % 2 == 1 and gathered > 1:
                ag_step(gathered)
                gathered -= 1

        elim[:, :rank] = gram / width
        elim[:, rank:] = jnp.where(row == col, 1.0, 0.0).astype(jnp.float32)
        cuts = [rank * j // (gathered + 1) for j in range(gathered + 2)]
        for j in range(gathered + 1):
            lax.fori_loop(cuts[j], cuts[j + 1], eliminate, 0)
            if gathered - j > 0:
                ag_step(gathered - j)
        done = elim[...]
        diagonal = jnp.sum(jnp.where(row == col, done[:, :rank], 0.0), axis=1, keepdims=True)
        inverse = done[:, rank:] / jnp.sqrt(diagonal)
        finish = arrived(inverse)
        for q, (offset, wide, order) in enumerate(streams):
            finish(place(q, 1), wide // 2)
        ag_step(0)
        for q, (offset, wide, order) in enumerate(streams):
            finish(place(q, 0) + (1 - bit_of(order[0])) * (wide // 2), wide // 2)
        for q in range(count):
            for s in range(k):
                rs_copy(q, s).wait_send()
                ag_copy(q, s).wait_send()
        for j in range(k + kt):
            gram_copy(j).wait_send()
        return inverse

    def halves(inverse):
        high = inverse.astype(jnp.bfloat16)
        low = (inverse - high.astype(jnp.float32)).astype(jnp.bfloat16)
        return jnp.concatenate([high, low], axis=0)

    def apply(inverse, whole, out):
        both = halves(inverse)

        def body(at):
            two = jnp.dot(both, whole[:, at], preferred_element_type=jnp.float32)
            out[:, at] = (two[:rank] + two[rank:]).astype(out.dtype)

        return body

    def core_sum(use):
        def copy(j):
            return remote(
                back_out.at[use, j], back_in.at[use, j],
                b_send.at[use, j], b_recv.at[use, j], targets[k + j],
            )

        total = back_out[use, 0]
        for j in range(kt):
            if j > 0:
                back_out[use, j] = total
            copy(j).start()
            copy(j).wait()
            total = total + back_in[use, j]
        return total

    back_out[0, 0] = proj_part[...]
    proj = core_sum(0).astype(jnp.bfloat16)
    act_load.wait()

    def multiply_left(at):
        left_part[:, at] = jnp.dot(
            proj, act[:, at], preferred_element_type=jnp.float32
        ).astype(left_part.dtype)

    back_out[1, 0] = jnp.zeros_like(back_out[1, 0])

    def left_arrived(inverse):
        def body(at):
            back_out[1, 0] += lax.dot_general(
                left_whole[:, at], act[:, at], (((1,), (1,)), ((), ())),
                preferred_element_type=jnp.float32,
            )

        return lambda start, size: tiles(start, size, body)

    left_inverse = cholqr(
        0, left_part, left_whole,
        lambda start, size: tiles(start, size, multiply_left), lambda: None, left_arrived,
    )

    total = core_sum(1)
    back = jnp.dot(
        left_inverse, total, precision=lax.Precision.HIGHEST,
        preferred_element_type=jnp.float32,
    ).astype(jnp.bfloat16)

    grad_load.wait()

    def multiply(at):
        right_part[:, at] = jnp.dot(
            back, grad[:, at], preferred_element_type=jnp.float32
        ).astype(right_part.dtype)

    def left_basis():
        tiles(0, left_out.shape[1], apply(left_inverse, left_whole, left_out))

    def right_arrived(inverse):
        body = apply(inverse, right_whole, right_out)
        return lambda start, size: tiles(start, size, body)

    cholqr(
        1, right_part, right_whole,
        lambda start, size: tiles(start, size, multiply), left_basis, right_arrived,
    )


def power_step(proj_part, activations, out_grads, n, tensors):
    rank, left_local = proj_part.shape[0], activations.shape[1]
    tokens, right_local = out_grads.shape
    k, kt = log2_of(n), log2_of(tensors)
    locals_ = (left_local, right_local)
    sides = [(plan_streams(local, n), local * tensors) for local in locals_]
    recv = [
        pltpu.VMEM((rank, wide >> (s + 1)), jnp.bfloat16)
        for streams, _ in sides
        for _, wide, _ in streams
        for s in range(k)
    ]
    dma = pltpu.SemaphoreType.DMA
    sems = []
    for streams, _ in sides:
        sems += [dma((len(streams), k))] * 4 + [dma((k + kt,))] * 2
    back_slots = max(kt, 1)
    return pl.pallas_call(
        functools.partial(power_kernel, n, tensors, sides),
        out_shape=(
            jax.ShapeDtypeStruct((rank, left_local), jnp.bfloat16),
            jax.ShapeDtypeStruct((rank, right_local), jnp.bfloat16),
        ),
        in_specs=[
            pl.BlockSpec(memory_space=pl.ANY),
            pl.BlockSpec(memory_space=pl.ANY),
            pl.BlockSpec(memory_space=pltpu.VMEM),
        ],
        out_specs=(
            pl.BlockSpec(memory_space=pltpu.VMEM),
            pl.BlockSpec(memory_space=pltpu.VMEM),
        ),
        scratch_shapes=recv + [
            pltpu.VMEM((rank, left_local), jnp.bfloat16),
            pltpu.VMEM((rank, left_local), jnp.bfloat16),
            pltpu.VMEM((rank, right_local), jnp.bfloat16),
            pltpu.VMEM((rank, right_local), jnp.bfloat16),
            pltpu.VMEM((2, k + kt, rank, rank), jnp.float32),
            pltpu.VMEM((2, k + kt, rank, rank), jnp.float32),
            pltpu.VMEM((rank, 2 * rank), jnp.float32),
            pltpu.VMEM((2, back_slots, rank, tokens), jnp.float32),
            pltpu.VMEM((2, back_slots, rank, tokens), jnp.float32),
            pltpu.VMEM((tokens, left_local), jnp.bfloat16),
            pltpu.VMEM((tokens, right_local), jnp.bfloat16),
        ] + sems + [dma((2, back_slots)), dma((2, back_slots)), dma((2,))],
        compiler_params=pltpu.CompilerParams(
            collective_id=0, has_side_effects=True,
            vmem_limit_bytes=52 * 1024 * 1024,
        ),
    )(activations, out_grads, proj_part)


def plain_cholqr(part, width):
    total = lax.psum(part, "dp")
    gram = lax.psum(
        jnp.dot(total, total.T, precision=lax.Precision.HIGHEST), "tensor"
    )
    chol = jnp.linalg.cholesky(gram / width)
    return jax.scipy.linalg.solve_triangular(chol, total, lower=True)


def plain_step(proj_part, activations, out_grads, tensors):
    proj = lax.psum(proj_part, "tensor").astype(jnp.bfloat16)
    left_part = jnp.dot(proj, activations, preferred_element_type=jnp.float32)
    left_basis = plain_cholqr(left_part, activations.shape[1] * tensors)
    back = lax.psum(
        lax.dot_general(
            activations, left_basis.astype(jnp.bfloat16), (((1,), (1,)), ((), ())),
            preferred_element_type=jnp.float32,
        ).astype(jnp.bfloat16),
        "tensor",
    )
    right_part = lax.dot_general(
        back, out_grads, (((0,), (0,)), ((), ())), preferred_element_type=jnp.float32
    )
    right_basis = plain_cholqr(right_part, out_grads.shape[1] * tensors)
    return left_basis, right_basis.astype(jnp.bfloat16)


def per_device(n, tensors, activations, out_grads, basis_in):
    proj_part = lax.dot_general(
        basis_in, out_grads, (((0,), (1,)), ((), ())), preferred_element_type=jnp.float32
    )
    k, kt = log2_of(n), log2_of(tensors)
    aligned = all(x.shape[1] % (n * LANES) == 0 for x in (activations, out_grads))
    if k is None or k < 2 or kt is None or not aligned:
        left_basis, right_basis = plain_step(proj_part, activations, out_grads, tensors)
    else:
        left_basis, right_basis = power_step(
            proj_part, activations, out_grads, n, tensors
        )
        left_basis = left_basis.astype(jnp.float32)
    return (left_basis.T, right_basis.T)


def solution(mesh):
    return jax.shard_map(
        functools.partial(per_device, mesh.shape["dp"], mesh.shape["tensor"]),
        mesh=mesh,
        in_specs=(P("dp", "tensor"), P("dp", "tensor"), P("tensor", None)),
        out_specs=(P("tensor", None), P("tensor", None)),
        check_vma=False,
    )
```

```python
import functools

import jax
import jax.numpy as jnp
from jax import lax
from jax.experimental import pallas as pl
from jax.experimental.pallas import tpu as pltpu
from jax.sharding import PartitionSpec as P

LANES = 128
STREAMS = 6


def log2_of(n):
    k = n.bit_length() - 1
    return k if n == 1 << k else None


def plan_streams(width, n):
    k = log2_of(n)
    units = width // (n * LANES)
    streams, offset = [], 0
    shares = [units // STREAMS + (q < units % STREAMS) for q in range(STREAMS)]
    if shares[-1] >= 2:
        shares[-1] -= 1
        shares[1] += 1
    for q, mine in enumerate(shares):
        if mine == 0:
            continue
        bits = list(range(k - 1))
        turn = q % (k - 1)
        order = bits[turn:] + bits[:turn] + [k - 1]
        streams.append((offset, mine * n * LANES, order))
        offset += mine * n * LANES
    return streams


def power_kernel(
    n, tensors, sides, act_hbm, grad_hbm, proj_part, left_out, right_out, *scratch
):
    k, kt = log2_of(n), log2_of(tensors)
    scratch = list(scratch)

    def take(count):
        taken = scratch[:count]
        del scratch[:count]
        return taken

    recvs = [take(len(streams) * k) for streams, _ in sides]
    left_whole, left_part, right_whole, right_part = take(4)
    gram_out, gram_in, elim, back_out, back_in, act, grad = take(7)
    side_sems = [take(6) for _ in sides]
    b_send, b_recv, load = take(3)
    rank = proj_part.shape[0]
    me = lax.axis_index("dp")
    core = lax.axis_index("tensor")

    act_load = pltpu.make_async_copy(act_hbm, act, load.at[0])
    grad_load = pltpu.make_async_copy(grad_hbm, grad, load.at[1])
    act_load.start()
    grad_load.start()

    def bit_of(b):
        return lax.rem(me // (1 << b), 2)

    def partner(b):
        return me + (1 << b) - 2 * (1 << b) * bit_of(b)

    def core_partner(b):
        bit = lax.rem(core // (1 << b), 2)
        return core + (1 << b) - 2 * (1 << b) * bit

    targets = [{"dp": partner(b)} for b in range(k)]
    targets += [{"tensor": core_partner(b)} for b in range(kt)]
    barrier = pltpu.get_barrier_semaphore()
    for target in targets:
        pl.semaphore_signal(barrier, inc=1, device_id=target, device_id_type=pl.DeviceIdType.MESH)
    pl.semaphore_wait(barrier, k + kt)

    def remote(src, dst, send, arrive, target):
        return pltpu.make_async_remote_copy(
            src_ref=src, dst_ref=dst, send_sem=send, recv_sem=arrive,
            device_id=target, device_id_type=pl.DeviceIdType.MESH,
        )

    def lanes(start, size):
        return pl.ds(pl.multiple_of(start, LANES), size)

    tile = n // 2 * LANES

    def tiles(start, size, body):
        def step(i, _):
            body(lanes(start + i * tile, tile))
            return 0

        lax.fori_loop(0, size // tile, step, 0)

    row = lax.broadcasted_iota(jnp.int32, (rank, rank), 0)
    col = lax.broadcasted_iota(jnp.int32, (rank, rank), 1)
    wide_lane = lax.broadcasted_iota(jnp.int32, (rank, 2 * rank), 1)
    tall_row = lax.broadcasted_iota(jnp.int32, (rank, 1), 0)

    def eliminate(i, _):
        x = elim[...]
        pivot_row = elim[pl.ds(i, 1), :]
        column = jnp.sum(jnp.where(wide_lane == i, x, 0.0), axis=1, keepdims=True)
        pivot = jnp.sum(jnp.where(wide_lane[:1] == i, pivot_row, 0.0), axis=1, keepdims=True)
        factor = jnp.where(tall_row > i, column / pivot, 0.0)
        elim[...] = x - factor * pivot_row
        return 0

    def cholqr(side, part, whole, produce, beside, arrived):
        streams, width = sides[side]
        recv = recvs[side]
        rs_send, rs_recv, ag_send, ag_recv, g_send, g_recv = side_sems[side]
        count = len(streams)

        def rs_copy(q, s):
            offset, wide, order = streams[q]
            half = wide >> (s + 1)
            src = part if s == 0 else recv[q * k + s - 1]
            start = (offset if s == 0 else 0) + (1 - bit_of(order[s])) * half
            return remote(
                src.at[:, lanes(start, half)], recv[q * k + s],
                rs_send.at[q, s], rs_recv.at[q, s], targets[order[s]],
            )

        for q, (offset, wide, order) in enumerate(streams):
            produce(offset + (1 - bit_of(order[0])) * (wide // 2), wide // 2)
            rs_copy(q, 0).start()
        for q, (offset, wide, order) in enumerate(streams):
            produce(offset + bit_of(order[0]) * (wide // 2), wide // 2)
        beside()
        for s in range(k):
            for q, (offset, wide, order) in enumerate(streams):
                rs_copy(q, s).wait_recv()
                half = wide >> (s + 1)
                step = wide // n
                src = part if s == 0 else recv[q * k + s - 1]
                start = (offset if s == 0 else 0) + bit_of(order[s]) * half
                here = recv[q * k + s]

                def add(i, _, src=src, here=here, start=start, step=step):
                    to = lanes(i * step, step)
                    mine = src[:, lanes(start + i * step, step)].astype(jnp.float32)
                    here[:, to] = (mine + here[:, to].astype(jnp.float32)).astype(here.dtype)
                    return 0

                lax.fori_loop(0, half // step, add, 0)
                if s + 1 < k:
                    rs_copy(q, s + 1).start()

        def place(q, s):
            offset, wide, order = streams[q]
            start = offset
            for j in range(s):
                start = start + bit_of(order[j]) * (wide >> (j + 1))
            return start

        def ag_copy(q, s):
            offset, wide, order = streams[q]
            here = whole.at[:, lanes(place(q, s + 1), wide >> (s + 1))]
            return remote(here, here, ag_send.at[q, s], ag_recv.at[q, s], targets[order[s]])

        gram = jnp.zeros((rank, rank), jnp.float32)
        for q, (offset, wide, order) in enumerate(streams):
            chunk = recv[q * k + k - 1][...]
            whole[:, lanes(place(q, k), wide // n)] = chunk
            ag_copy(q, k - 1).start()
            gram = gram + lax.dot_general(
                chunk, chunk, (((1,), (1,)), ((), ())), preferred_element_type=jnp.float32
            )

        def ag_step(s):
            for q in range(count):
                ag_copy(q, s).wait_recv()
                if s > 0:
                    ag_copy(q, s - 1).start()

        def gram_copy(j):
            return remote(
                gram_out.at[side, j], gram_in.at[side, j], g_send.at[j], g_recv.at[j],
                targets[(j + k) % (k + kt)],
            )

        gram_out[side, 0] = gram
        gram_copy(0).start()
        gathered = k - 1
        for j in range(k + kt):
            gram_copy(j).wait_recv()
            gram = gram + gram_in[side, j]
            if j + 1 < k + kt:
                gram_out[side, j + 1] = gram
                gram_copy(j + 1).start()
            if j % 2 == 1 and gathered > 1:
                ag_step(gathered)
                gathered -= 1

        elim[:, :rank] = gram / width
        elim[:, rank:] = jnp.where(row == col, 1.0, 0.0).astype(jnp.float32)
        cuts = [rank * j // (gathered + 1) for j in range(gathered + 2)]
        for j in range(gathered + 1):
            lax.fori_loop(cuts[j], cuts[j + 1], eliminate, 0)
            if gathered - j > 0:
                ag_step(gathered - j)
        done = elim[...]
        diagonal = jnp.sum(jnp.where(row == col, done[:, :rank], 0.0), axis=1, keepdims=True)
        inverse = done[:, rank:] / jnp.sqrt(diagonal)
        finish = arrived(inverse)
        for q, (offset, wide, order) in enumerate(streams):
            finish(place(q, 1), wide // 2)
        ag_step(0)
        for q, (offset, wide, order) in enumerate(streams):
            finish(place(q, 0) + (1 - bit_of(order[0])) * (wide // 2), wide // 2)
        for q in range(count):
            for s in range(k):
                rs_copy(q, s).wait_send()
                ag_copy(q, s).wait_send()
        for j in range(k + kt):
            gram_copy(j).wait_send()
        return inverse

    def halves(inverse):
        high = inverse.astype(jnp.bfloat16)
        low = (inverse - high.astype(jnp.float32)).astype(jnp.bfloat16)
        return jnp.concatenate([high, low], axis=0)

    def apply(inverse, whole, out):
        both = halves(inverse)

        def body(at):
            two = jnp.dot(both, whole[:, at], preferred_element_type=jnp.float32)
            out[:, at] = (two[:rank] + two[rank:]).astype(out.dtype)

        return body

    def core_sum(use):
        def copy(j):
            return remote(
                back_out.at[use, j], back_in.at[use, j],
                b_send.at[use, j], b_recv.at[use, j], targets[k + j],
            )

        total = back_out[use, 0]
        for j in range(kt):
            if j > 0:
                back_out[use, j] = total
            copy(j).start()
            copy(j).wait()
            total = total + back_in[use, j]
        return total

    back_out[0, 0] = proj_part[...]
    proj = core_sum(0).astype(jnp.bfloat16)
    act_load.wait()

    def multiply_left(at):
        left_part[:, at] = jnp.dot(
            proj, act[:, at], preferred_element_type=jnp.float32
        ).astype(left_part.dtype)

    back_out[1, 0] = jnp.zeros_like(back_out[1, 0])

    def left_arrived(inverse):
        def body(at):
            back_out[1, 0] += lax.dot_general(
                left_whole[:, at], act[:, at], (((1,), (1,)), ((), ())),
                preferred_element_type=jnp.float32,
            )

        return lambda start, size: tiles(start, size, body)

    left_inverse = cholqr(
        0, left_part, left_whole,
        lambda start, size: tiles(start, size, multiply_left), lambda: None, left_arrived,
    )

    total = core_sum(1)
    back = jnp.dot(
        left_inverse, total, precision=lax.Precision.HIGHEST,
        preferred_element_type=jnp.float32,
    ).astype(jnp.bfloat16)

    grad_load.wait()

    def multiply(at):
        right_part[:, at] = jnp.dot(
            back, grad[:, at], preferred_element_type=jnp.float32
        ).astype(right_part.dtype)

    def left_basis():
        tiles(0, left_out.shape[1], apply(left_inverse, left_whole, left_out))

    def right_arrived(inverse):
        body = apply(inverse, right_whole, right_out)
        return lambda start, size: tiles(start, size, body)

    cholqr(
        1, right_part, right_whole,
        lambda start, size: tiles(start, size, multiply), left_basis, right_arrived,
    )


def power_step(proj_part, activations, out_grads, n, tensors):
    rank, left_local = proj_part.shape[0], activations.shape[1]
    tokens, right_local = out_grads.shape
    k, kt = log2_of(n), log2_of(tensors)
    locals_ = (left_local, right_local)
    sides = [(plan_streams(local, n), local * tensors) for local in locals_]
    recv = [
        pltpu.VMEM((rank, wide >> (s + 1)), jnp.bfloat16)
        for streams, _ in sides
        for _, wide, _ in streams
        for s in range(k)
    ]
    dma = pltpu.SemaphoreType.DMA
    sems = []
    for streams, _ in sides:
        sems += [dma((len(streams), k))] * 4 + [dma((k + kt,))] * 2
    back_slots = max(kt, 1)
    return pl.pallas_call(
        functools.partial(power_kernel, n, tensors, sides),
        out_shape=(
            jax.ShapeDtypeStruct((rank, left_local), jnp.bfloat16),
            jax.ShapeDtypeStruct((rank, right_local), jnp.bfloat16),
        ),
        in_specs=[
            pl.BlockSpec(memory_space=pl.ANY),
            pl.BlockSpec(memory_space=pl.ANY),
            pl.BlockSpec(memory_space=pltpu.VMEM),
        ],
        out_specs=(
            pl.BlockSpec(memory_space=pltpu.VMEM),
            pl.BlockSpec(memory_space=pltpu.VMEM),
        ),
        scratch_shapes=recv + [
            pltpu.VMEM((rank, left_local), jnp.bfloat16),
            pltpu.VMEM((rank, left_local), jnp.bfloat16),
            pltpu.VMEM((rank, right_local), jnp.bfloat16),
            pltpu.VMEM((rank, right_local), jnp.bfloat16),
            pltpu.VMEM((2, k + kt, rank, rank), jnp.float32),
            pltpu.VMEM((2, k + kt, rank, rank), jnp.float32),
            pltpu.VMEM((rank, 2 * rank), jnp.float32),
            pltpu.VMEM((2, back_slots, rank, tokens), jnp.float32),
            pltpu.VMEM((2, back_slots, rank, tokens), jnp.float32),
            pltpu.VMEM((tokens, left_local), jnp.bfloat16),
            pltpu.VMEM((tokens, right_local), jnp.bfloat16),
        ] + sems + [dma((2, back_slots)), dma((2, back_slots)), dma((2,))],
        compiler_params=pltpu.CompilerParams(
            collective_id=0, has_side_effects=True,
            vmem_limit_bytes=36 * 1024 * 1024,
        ),
    )(activations, out_grads, proj_part)


def plain_cholqr(part, width):
    total = lax.psum(part, "dp")
    gram = lax.psum(
        jnp.dot(total, total.T, precision=lax.Precision.HIGHEST), "tensor"
    )
    chol = jnp.linalg.cholesky(gram / width)
    return jax.scipy.linalg.solve_triangular(chol, total, lower=True)


def plain_step(proj_part, activations, out_grads, tensors):
    proj = lax.psum(proj_part, "tensor").astype(jnp.bfloat16)
    left_part = jnp.dot(proj, activations, preferred_element_type=jnp.float32)
    left_basis = plain_cholqr(left_part, activations.shape[1] * tensors)
    back = lax.psum(
        lax.dot_general(
            activations, left_basis.astype(jnp.bfloat16), (((1,), (1,)), ((), ())),
            preferred_element_type=jnp.float32,
        ).astype(jnp.bfloat16),
        "tensor",
    )
    right_part = lax.dot_general(
        back, out_grads, (((0,), (0,)), ((), ())), preferred_element_type=jnp.float32
    )
    right_basis = plain_cholqr(right_part, out_grads.shape[1] * tensors)
    return left_basis, right_basis.astype(jnp.bfloat16)


def per_device(n, tensors, activations, out_grads, basis_in):
    proj_part = lax.dot_general(
        basis_in, out_grads, (((0,), (1,)), ((), ())), preferred_element_type=jnp.float32
    )
    k, kt = log2_of(n), log2_of(tensors)
    aligned = all(x.shape[1] % (n * LANES) == 0 for x in (activations, out_grads))
    if k is None or k < 2 or kt is None or not aligned:
        left_basis, right_basis = plain_step(proj_part, activations, out_grads, tensors)
    else:
        left_basis, right_basis = power_step(
            proj_part, activations, out_grads, n, tensors
        )
        left_basis = left_basis.astype(jnp.float32)
    return (left_basis.T, right_basis.T)


def solution(mesh):
    return jax.shard_map(
        functools.partial(per_device, mesh.shape["dp"], mesh.shape["tensor"]),
        mesh=mesh,
        in_specs=(P("dp", "tensor"), P("dp", "tensor"), P("tensor", None)),
        out_specs=(P("tensor", None), P("tensor", None)),
        check_vma=False,
    )
```
